32 devices in a mesh: dp: 8 (over z, y), tensor: 4 (over x, core).
Axes of the slice: x: 2, y: 2, z: 4, core: 2. Of those that a mesh axis runs over, the one named last changes fastest.
Arguments:
- hidden_in: bfloat16 [16384, 1024], P(('dp', 'tensor')), may hold values from -6 to 6
- grad_out: bfloat16 [16384, 1024], P(('dp', 'tensor')), may hold values from -6 to 6
- seq_lengths: int32 [8, 4], P('dp'), may hold values from 0 to 1024, as said below
- qkv_weight: float32 [1024, 3072], P('dp', 'tensor'), may hold values from -0.25 to 0.25
- qkv_first: float32 [1024, 3072], P('dp', 'tensor'), may hold values from -80 to 80
- qkv_second: float32 [1024, 3072], P('dp', 'tensor'), may hold values from 8.192 to 131.072
- dense_weight: float32 [1024, 1024], P('tensor', 'dp'), may hold values from -0.75 to 0.75
- dense_first: float32 [1024, 1024], P('tensor', 'dp'), may hold values from -14 to 14
- dense_second: float32 [1024, 1024], P('tensor', 'dp'), may hold values from 0.180224 to 2.94912
- up_weight: float32 [1024, 4096], P('dp', 'tensor'), may hold values from -0.1875 to 0.1875
- up_first: float32 [1024, 4096], P('dp', 'tensor'), may hold values from -40 to 40
- up_second: float32 [1024, 4096], P('dp', 'tensor'), may hold values from 2.048 to 32.768
- down_weight: float32 [4096, 1024], P('tensor', 'dp'), may hold values from -0.09375 to 0.09375
- down_first: float32 [4096, 1024], P('tensor', 'dp'), may hold values from -40 to 40
- down_second: float32 [4096, 1024], P('tensor', 'dp'), may hold values from 2.048 to 32.768
- qkv_bias: float32 [3072], P(('tensor', 'dp')), may hold values from -4 to 4
- qkv_bias_first: float32 [3072], P(('tensor', 'dp')), may hold values from -80 to 80
- qkv_bias_second: float32 [3072], P(('tensor', 'dp')), may hold values from 8.192 to 131.072
- up_bias: float32 [4096], P(('tensor', 'dp')), may hold values from -4 to 4
- up_bias_first: float32 [4096], P(('tensor', 'dp')), may hold values from -40 to 40
- up_bias_second: float32 [4096], P(('tensor', 'dp')), may hold values from 2.048 to 32.768
- vectors: float32 [6, 1024], P(None, 'dp'), may hold values from -1.5 to 1.5
- vectors_first: float32 [6, 1024], P(None, 'dp'), may hold values from -80 to 80
- vectors_second: float32 [6, 1024], P(None, 'dp'), may hold values from 8.192 to 131.072
Outputs:
- hidden_out: bfloat16 [16384, 1024], P(('dp', 'tensor'))
- hidden_grad: float32 [16384, 1024], P(('dp', 'tensor'))
- qkv_weight_new: float32 [1024, 3072], P('dp', 'tensor')
- qkv_first_new: float32 [1024, 3072], P('dp', 'tensor')
- qkv_second_new: float32 [1024, 3072], P('dp', 'tensor')
- dense_weight_new: float32 [1024, 1024], P('tensor', 'dp')
- dense_first_new: float32 [1024, 1024], P('tensor', 'dp')
- dense_second_new: float32 [1024, 1024], P('tensor', 'dp')
- up_weight_new: float32 [1024, 4096], P('dp', 'tensor')
- up_first_new: float32 [1024, 4096], P('dp', 'tensor')
- up_second_new: float32 [1024, 4096], P('dp', 'tensor')
- down_weight_new: float32 [4096, 1024], P('tensor', 'dp')
- down_first_new: float32 [4096, 1024], P('tensor', 'dp')
- down_second_new: float32 [4096, 1024], P('tensor', 'dp')
- qkv_bias_new: float32 [3072], P(('tensor', 'dp'))
- qkv_bias_first_new: float32 [3072], P(('tensor', 'dp'))
- qkv_bias_second_new: float32 [3072], P(('tensor', 'dp'))
- up_bias_new: float32 [4096], P(('tensor', 'dp'))
- up_bias_first_new: float32 [4096], P(('tensor', 'dp'))
- up_bias_second_new: float32 [4096], P(('tensor', 'dp'))
- vectors_new: float32 [6, 1024], P(None, 'dp')
- vectors_first_new: float32 [6, 1024], P(None, 'dp')
- vectors_second_new: float32 [6, 1024], P(None, 'dp')
The draws below stay inside these ranges and needn't reach their ends.
Inputs may be any that keep to these rules, and one draw needn't show every extreme that they name: `seq_lengths`: each row sums to at most 2048; the slots after the last sequence are padding; some row holds a sequence of exactly 1024; a slot may be empty.
All inputs are finite; a program needn't handle non-finite values.
Results may differ from the reference program's by a relative error of at most 0.012.
The reference program's roundings to bfloat16 on the way count: a program that leaves them out, or rounds other values in their place, can miss the bound.
Values may be sent and summed in bfloat16 or wider, within the bound.
A program may use at most 192 MiB of HBM per device.

```python
import math
import jax
import jax.numpy as jnp
from jax import lax

D = 1024
H = 16
HD = 64
ROT = 16
FF = 4096
TOK_DEV = 2048
SEQS = 4
STEP = 10
MAXLEN = 1024
QB = 512
TOKENS = 16384
N_DP = 8


def draw_seq_lengths(key, part):
    key = jax.random.fold_in(key, 11)
    key_top, key_raw, key_pick = jax.random.split(key, 3)
    ceiling = jax.random.randint(key_top, (N_DP, 1), MAXLEN // 8, MAXLEN + 1)
    raw = jax.random.randint(key_raw, (N_DP, SEQS), 0, 1 << 20) % ceiling + 1
    chosen = jax.random.randint(key_pick, (), 0, N_DP)
    row_ids = jnp.arange(N_DP)[:, None]
    col_ids = jnp.arange(SEQS)[None, :]
    raw = jnp.where((row_ids == chosen) & (col_ids == 0), MAXLEN, raw)
    before = jnp.cumsum(raw, 1) - raw
    room = jnp.maximum(TOK_DEV - before, 0)
    return jnp.minimum(raw, room).astype(jnp.int32)


def draw_vectors(key, part):
    key = jax.random.fold_in(key, 12)
    key_gain, key_shift = jax.random.split(key)
    gains = jax.random.uniform(key_gain, (6, D), jnp.float32, 0.5, 1.5)
    shifts = jnp.clip(0.3 * jax.random.normal(key_shift, (6, D), jnp.float32), -1.2, 1.2)
    row_ids = jnp.arange(6)[:, None]
    return jnp.where((row_ids == 0) | (row_ids == 2), gains, shifts)


def block_scale(stream_key, shape, shards, least, largest):
    loudness = 1.0
    for dim, parts in shards:
        draws = jax.random.uniform(jax.random.fold_in(jax.random.fold_in(stream_key, 6), dim), (parts,), jnp.float32, least / len(shards), largest / len(shards))
        loudness = loudness * jnp.repeat(jnp.exp(draws), shape[dim] // parts).reshape((-1,) + (1,) * (len(shape) - 1 - dim))
    return loudness


def noise(key, dims, width, limit, shards=(), kind=jnp.bfloat16):
    drawn = width * jax.random.normal(key, dims, jnp.float32)
    if shards:
        drawn = drawn * block_scale(key, dims, shards, -0.22, 0.18)
    return jnp.clip(drawn, -limit, limit).astype(kind)


def setup_inputs(seed: int = 0) -> dict:
    key_list = jax.random.split(jax.random.key(seed), 25)
    return {
        "hidden_in": noise(key_list[0], (TOKENS, D), 1.0, 6.0, ((0, 32),)),
        "grad_out": noise(key_list[1], (TOKENS, D), 1.0, 6.0, ((0, 32),)),
        "seq_lengths": draw_seq_lengths(jax.random.fold_in(key_list[24], 71), 0),
        "qkv_weight": noise(key_list[3], (D, 3 * D), (D // 2) ** -0.5, 0.25, ((0, 8), (1, 4)), jnp.float32),
        "qkv_first": noise(key_list[4], (D, 3 * D), (0.11 * TOKENS ** 0.5), 80.0, ((0, 8), (1, 4)), jnp.float32),
        "qkv_second": jnp.clip(jnp.exp(math.log(131.072) - 2.7725887 * jax.random.uniform(key_list[5], (D, 3 * D), jnp.float32) ** block_scale(key_list[5], (D, 3 * D), ((0, 8), (1, 4)), -0.2, 0.2)), 8.192, 131.072),
        "dense_weight": noise(key_list[6], (D, D), (D // 16) ** -0.5, 0.75, ((0, 4), (1, 8)), jnp.float32),
        "dense_first": noise(key_list[7], (D, D), (0.017 * TOKENS ** 0.5), 14.0, ((0, 4), (1, 8)), jnp.float32),
        "dense_second": jnp.clip(jnp.exp(math.log(2.94912) - 2.7950616 * jax.random.uniform(key_list[8], (D, D), jnp.float32) ** block_scale(key_list[8], (D, D), ((0, 4), (1, 8)), -0.2, 0.2)), 0.180224, 2.94912),
        "up_weight": noise(key_list[9], (D, FF), D ** -0.5, 0.1875, ((0, 8), (1, 4)), jnp.float32),
        "up_first": noise(key_list[10], (D, FF), (0.055 * TOKENS ** 0.5), 40.0, ((0, 8), (1, 4)), jnp.float32),
        "up_second": jnp.clip(jnp.exp(math.log(32.768) - 2.7725887 * jax.random.uniform(key_list[11], (D, FF), jnp.float32) ** block_scale(key_list[11], (D, FF), ((0, 8), (1, 4)), -0.2, 0.2)), 2.048, 32.768),
        "down_weight": noise(key_list[12], (FF, D), FF ** -0.5, 0.09375, ((0, 4), (1, 8)), jnp.float32),
        "down_first": noise(key_list[13], (FF, D), (0.055 * TOKENS ** 0.5), 40.0, ((0, 4), (1, 8)), jnp.float32),
        "down_second": jnp.clip(jnp.exp(math.log(32.768) - 2.7725887 * jax.random.uniform(key_list[14], (FF, D), jnp.float32) ** block_scale(key_list[14], (FF, D), ((0, 4), (1, 8)), -0.2, 0.2)), 2.048, 32.768),
        "qkv_bias": noise(key_list[15], (3 * D,), 0.3, 4.0, ((0, 32),), jnp.float32),
        "qkv_bias_first": noise(key_list[16], (3 * D,), (0.11 * TOKENS ** 0.5), 80.0, ((0, 32),), jnp.float32),
        "qkv_bias_second": jnp.clip(jnp.exp(math.log(131.072) - 2.7725887 * jax.random.uniform(key_list[17], (3 * D,), jnp.float32) ** block_scale(key_list[17], (3 * D,), ((0, 32),), -0.2, 0.2)), 8.192, 131.072),
        "up_bias": noise(key_list[18], (FF,), 0.3, 4.0, ((0, 32),), jnp.float32),
        "up_bias_first": noise(key_list[19], (FF,), (0.055 * TOKENS ** 0.5), 40.0, ((0, 32),), jnp.float32),
        "up_bias_second": jnp.clip(jnp.exp(math.log(32.768) - 2.7725887 * jax.random.uniform(key_list[20], (FF,), jnp.float32) ** block_scale(key_list[20], (FF,), ((0, 32),), -0.2, 0.2)), 2.048, 32.768),
        "vectors": draw_vectors(jax.random.fold_in(key_list[24], 71), 0),
        "vectors_first": noise(key_list[22], (6, D), (0.11 * TOKENS ** 0.5), 80.0, ((1, 8),), jnp.float32),
        "vectors_second": jnp.clip(jnp.exp(math.log(131.072) - 2.7725887 * jax.random.uniform(key_list[23], (6, D), jnp.float32) ** block_scale(key_list[23], (6, D), ((1, 8),), -0.2, 0.2)), 8.192, 131.072),
    }


@jax.custom_vjp
def low(v):
    return lax.optimization_barrier(v.astype(jnp.bfloat16)).astype(jnp.float32)

@jax.custom_vjp
def low_back(v):
    return v

def low_keep(v):
    return (low(v), None)

def low_pass(kept, grad):
    return (grad,)

def back_keep(v):
    return (v, None)

def back_low(kept, grad):
    return (low(grad),)
low.defvjp(low_keep, low_pass)
low_back.defvjp(back_keep, back_low)

def layout(lengths):
    ends = jnp.cumsum(lengths).astype(jnp.int32)
    starts = (ends - lengths).astype(jnp.int32)
    place = jnp.arange(TOK_DEV, dtype=jnp.int32)
    segment = lax.optimization_barrier(jnp.sum((place[:, None] >= ends[None, :]).astype(jnp.int32), 1)).astype(jnp.int32)
    slots = jnp.arange(SEQS, dtype=jnp.int32)
    begin = lax.optimization_barrier(jnp.sum(jnp.where(segment[:, None] == slots[None, :], starts[None, :], 0), 1)).astype(jnp.int32)
    begin = jnp.where(segment == SEQS, ends[SEQS - 1], begin)
    position = (place - begin).astype(jnp.int32)
    live = segment < SEQS
    return (segment, position, live)

def layer_norm(values, gain, shift):
    center = values - lax.optimization_barrier(jnp.mean(values, -1, keepdims=True))
    spread = lax.optimization_barrier(jnp.mean(center * center, -1, keepdims=True))
    return center * lax.rsqrt(spread + 1e-05) * gain + shift

def angles(position):
    half = ROT // 2
    freq = jnp.exp(-math.log(10000.0) * jnp.arange(half, dtype=jnp.float32) * 2.0 / ROT)
    turn = position.astype(jnp.float32)[:, None] * freq[None, :]
    return (jnp.cos(turn), jnp.sin(turn))

def rotate(part, cosine, sine):
    half = ROT // 2
    first = part[..., :half]
    second = part[..., half:ROT]
    cos_b = cosine[:, None, :]
    sin_b = sine[:, None, :]
    return jnp.concatenate([first * cos_b - second * sin_b, second * cos_b + first * sin_b, part[..., ROT:]], -1)

def attend(items, keys, values, seg_keys, place_keys):
    queries, seg_query, place_query, live_query = items
    scores = low_back(jnp.einsum('qhd,khd->hqk', queries, keys, precision=lax.Precision.HIGHEST) * HD ** (-0.5))
    allowed = (seg_query[:, None] == seg_keys[None, :]) & (place_keys[None, :] <= place_query[:, None])
    scores = jnp.where(allowed[None], scores, -1000000000.0)
    peak = lax.optimization_barrier(jnp.max(scores, -1, keepdims=True))
    log_total = peak + jnp.log(lax.optimization_barrier(jnp.sum(jnp.exp(scores - peak), -1, keepdims=True)))
    prob = low(jnp.exp(scores - log_total))
    result = jnp.einsum('hqk,khd->qhd', prob, values, precision=lax.Precision.HIGHEST)
    return result * live_query.astype(jnp.float32)[:, None, None]

def group_forward(params, x_float, segment, position, live):
    w_qkv, w_dense, w_up, w_down, b_qkv, b_up, vecs = params
    norm_one = low(layer_norm(x_float, vecs[0], vecs[1]))
    norm_two = low(layer_norm(x_float, vecs[2], vecs[3]))
    qkv = low_back(jnp.dot(norm_one, low(w_qkv), precision=lax.Precision.HIGHEST) + b_qkv)
    qkv = qkv.reshape(TOK_DEV, H, 3, HD)
    cosine, sine = angles(position)
    query = low(rotate(qkv[:, :, 0], cosine, sine))
    key_rot = low(rotate(qkv[:, :, 1], cosine, sine))
    value = low(qkv[:, :, 2])
    place = jnp.arange(TOK_DEV, dtype=jnp.int32)
    blocks = TOK_DEV // QB
    items = (query.reshape(blocks, QB, H, HD), segment.reshape(blocks, QB), place.reshape(blocks, QB), live.reshape(blocks, QB))
    block_fn = jax.checkpoint(lambda piece: attend(piece, key_rot, value, segment, place))
    attended = lax.map(block_fn, items).reshape(TOK_DEV, H * HD)
    attended = low_back(low(attended))
    upward = low_back(jnp.dot(norm_two, low(w_up), precision=lax.Precision.HIGHEST) + b_up)
    activated = low(jax.nn.gelu(upward, approximate=False))
    mixed = jnp.dot(attended, low(w_dense), precision=lax.Precision.HIGHEST) + jnp.dot(activated, low(w_down), precision=lax.Precision.HIGHEST)
    return x_float + mixed + vecs[4] + vecs[5]

def adamw(weight, grad, first, second, rate, decay):
    first_new = 0.9 * first + 0.1 * grad
    second_new = 0.999 * second + 0.001 * grad * grad
    moment_hat = first_new / (1.0 - 0.9 ** STEP)
    square_hat = second_new / (1.0 - 0.999 ** STEP)
    weight_new = weight - rate * (moment_hat / (jnp.sqrt(square_hat) + 1e-08) + decay * weight)
    return (weight_new, first_new, second_new)

def reference(hidden_in, grad_out, seq_lengths, qkv_weight, qkv_first, qkv_second, dense_weight, dense_first, dense_second, up_weight, up_first, up_second, down_weight, down_first, down_second, qkv_bias, qkv_bias_first, qkv_bias_second, up_bias, up_bias_first, up_bias_second, vectors, vectors_first, vectors_second):
    params = (qkv_weight, dense_weight, up_weight, down_weight, qkv_bias, up_bias, vectors)
    groups_x = hidden_in.reshape(N_DP, TOK_DEV, D)
    groups_dy = grad_out.reshape(N_DP, TOK_DEV, D)
    totals = jax.tree.map(jnp.zeros_like, params)

    def one_group(carry, items):
        x_group, dy_group, lengths = items
        segment, position, live = layout(lengths)
        x_float = x_group.astype(jnp.float32)

        def forward(param_set, x_values):
            return group_forward(param_set, x_values, segment, position, live)
        result, pullback = jax.vjp(forward, params, x_float)
        cotangent = jnp.where(live[:, None], dy_group.astype(jnp.float32), jnp.zeros((), jnp.float32))
        grads, grad_x = pullback(cotangent)
        carry = jax.tree.map(lambda left_val, right_val: left_val + right_val, carry, grads)
        return (carry, (result.astype(jnp.bfloat16), grad_x))
    grads, (outputs, grad_inputs) = lax.scan(one_group, totals, (groups_x, groups_dy, seq_lengths))
    g_qkv, g_dense, g_up, g_down, g_qbias, g_ubias, g_vecs = grads
    qkv_set = adamw(qkv_weight, g_qkv, qkv_first, qkv_second, 2.0 * (D // 2) ** (-0.5), 0.01)
    dense_set = adamw(dense_weight, g_dense, dense_first, dense_second, 2.0 * (D // 16) ** (-0.5), 0.01)
    up_set = adamw(up_weight, g_up, up_first, up_second, 2.0 * D ** (-0.5), 0.01)
    down_set = adamw(down_weight, g_down, down_first, down_second, 2.0 * FF ** (-0.5), 0.01)
    qbias_set = adamw(qkv_bias, g_qbias, qkv_bias_first, qkv_bias_second, 0.6, 0.0)
    ubias_set = adamw(up_bias, g_ubias, up_bias_first, up_bias_second, 0.6, 0.0)
    vec_set = adamw(vectors, g_vecs, vectors_first, vectors_second, 0.6, 0.0)
    return (outputs.reshape(TOKENS, D), grad_inputs.reshape(TOKENS, D), qkv_set[0], qkv_set[1], qkv_set[2], dense_set[0], dense_set[1], dense_set[2], up_set[0], up_set[1], up_set[2], down_set[0], down_set[1], down_set[2], qbias_set[0], qbias_set[1], qbias_set[2], ubias_set[0], ubias_set[1], ubias_set[2], vec_set[0], vec_set[1], vec_set[2])
```

```python
import functools
import math

import jax
import jax.numpy as jnp
from jax import lax
from jax.experimental import pallas as pl
from jax.experimental.pallas import tpu as pltpu
from jax.sharding import PartitionSpec as P

D = 1024
HD = 64
ROT = 16
FF = 4096
TOK_DEV = 2048
SEQS = 4
STEP = 10
QB = 256
LOW = jnp.bfloat16
F32 = jnp.float32


def dims(a, b):
    return (((a,), (b,)), ((), ()))


def dot(left, right, a, b):
    return lax.dot_general(left, right, dims(a, b), preferred_element_type=F32)


def layout(lengths):
    ends = jnp.cumsum(lengths)
    starts = ends - lengths
    place = jnp.arange(TOK_DEV, dtype=jnp.int32)
    segment = jnp.sum((place[:, None] >= ends[None, :]).astype(jnp.int32), 1)
    slots = jnp.arange(SEQS, dtype=jnp.int32)
    begin = jnp.sum(jnp.where(segment[:, None] == slots[None, :], starts[None, :], 0), 1)
    begin = jnp.where(segment == SEQS, ends[SEQS - 1], begin)
    return (begin, place - begin, segment < SEQS, ends[SEQS - 1])


def turn_tables(position):
    half = ROT // 2
    freq = jnp.exp(-math.log(10000.0) * jnp.arange(half, dtype=F32) * 2.0 / ROT)
    turn = freq[:, None] * position.astype(F32)[None, :]
    lane = jnp.arange(128) % HD
    pick = (lane[None, :] % half == jnp.arange(half)[:, None]) & (lane[None, :] < ROT)
    sign = jnp.where(lane < half, -1.0, 1.0)
    spread = functools.partial(jnp.einsum, "ft,fc->tc", precision=lax.Precision.HIGHEST)
    cosine = spread(jnp.cos(turn), pick.astype(F32)) + (lane >= ROT).astype(F32)
    sine = spread(jnp.sin(turn), pick.astype(F32) * sign)
    return (cosine, sine)


def spin(part, cosine, sine, lane, back):
    half = ROT // 2
    width = part.shape[1]
    copies = width // 128
    cos_w = jnp.concatenate([cosine] * copies, 1)
    sin_w = jnp.concatenate([sine] * copies, 1)
    other = jnp.where(
        lane % HD < half, pltpu.roll(part, width - half, 1), pltpu.roll(part, half, 1)
    )
    return part * cos_w - other * sin_w if back else part * cos_w + other * sin_w


def allowed_pairs(i, j, begin_row):
    key_place = j * QB + lax.broadcasted_iota(jnp.int32, (QB, QB), 0)
    query_place = i * QB + lax.broadcasted_iota(jnp.int32, (QB, QB), 1)
    return (key_place >= begin_row) & (key_place <= query_place)


def rows_of(i):
    return pl.ds(pl.multiple_of(i * QB, QB), QB)


def forward_kernel(
    heads, info, qkv, cos_t, sin_t, begin, pick, out, lse, q_out, k_out, v_out, score, v_turn
):
    width = heads * HD
    blocks = qkv.shape[0] // QB
    lane = lax.broadcasted_iota(jnp.int32, (QB, width), 1)
    used = info[blocks]

    def prepare(i, carry):
        at = rows_of(i)
        cosine, sine = cos_t[at, :], sin_t[at, :]
        query = spin(qkv[at, :width], cosine, sine, lane, False).astype(LOW)
        q_out[at, :] = (query.astype(F32) * HD ** (-0.5)).astype(LOW)
        k_out[at, :] = spin(qkv[at, width : 2 * width], cosine, sine, lane, False).astype(LOW)
        value = qkv[at, 2 * width :]
        v_out[at, :] = value.astype(LOW)
        v_turn[i] = value.T.astype(LOW)
        return carry

    lax.fori_loop(0, blocks, prepare, 0)

    def block(i, carry):
        at = rows_of(i)
        low = info[i]
        begin_row = begin[i][0:1]
        query = q_out[at, :]
        parts = [query * pick[h : h + 1, :] for h in range(heads)]

        def first(j, peaks):
            keys = k_out[rows_of(j), :]
            allowed = allowed_pairs(i, j, begin_row)
            new = []
            for h in range(heads):
                value = jnp.where(allowed, dot(keys, parts[h], 1, 1), -1000000000.0)
                score[h, j] = value
                new.append(jnp.maximum(peaks[h], jnp.max(value, 0, keepdims=True)))
            return tuple(new)

        peaks = lax.fori_loop(
            low, i + 1, first, tuple(jnp.full((1, QB), -2e9, F32) for _ in range(heads))
        )

        def second(j, state):
            totals, sums = state
            new_totals, new_sums = [], []
            for h in range(heads):
                prob = jnp.exp(score[h, j] - peaks[h])
                new_sums.append(sums[h] + jnp.sum(prob, 0, keepdims=True))
                v_part = v_turn[j, h * HD : (h + 1) * HD, :]
                new_totals.append(totals[h] + dot(v_part, prob.astype(LOW), 1, 0))
            return (tuple(new_totals), tuple(new_sums))

        totals, sums = lax.fori_loop(
            low,
            i + 1,
            second,
            (
                tuple(jnp.zeros((HD, QB), F32) for _ in range(heads)),
                tuple(jnp.zeros((1, QB), F32) for _ in range(heads)),
            ),
        )
        live = (i * QB + lax.broadcasted_iota(jnp.int32, (1, QB), 1) < used).astype(F32)
        result = jnp.concatenate([totals[h] * (live / sums[h]) for h in range(heads)], 0)
        out[at, :] = result.T.astype(LOW)
        logs = [peaks[h] + jnp.log(sums[h]) for h in range(heads)]
        lse[i] = jnp.concatenate(logs + [jnp.zeros((8 - heads, QB), F32)], 0)
        return carry

    def blank(i, carry):
        out[rows_of(i), :] = jnp.zeros((QB, width), LOW)
        lse[i] = jnp.zeros((8, QB), F32)
        return carry

    count = info[blocks + 1]
    lax.fori_loop(0, count, block, 0)
    lax.fori_loop(count, blocks, blank, 0)


def backward_kernel(
    heads, info, q_in, k_in, v_in, out, grad_out, lse, cos_t, sin_t, begin, pick, grad, key_sum, value_sum
):
    width = heads * HD
    blocks = q_in.shape[0] // QB
    lane = lax.broadcasted_iota(jnp.int32, (QB, width), 1)
    used = info[blocks]
    count = info[blocks + 1]
    key_sum[...] = jnp.zeros_like(key_sum)
    value_sum[...] = jnp.zeros_like(value_sum)

    def block(i, carry):
        at = rows_of(i)
        begin_row = begin[i][0:1]
        row = i * QB + lax.broadcasted_iota(jnp.int32, (QB, width), 0)
        cot = jnp.where(row < used, grad_out[at, :].astype(F32), 0.0)
        spread = (cot * out[at, :].astype(F32)).T
        deltas = [
            jnp.sum(spread[h * HD : (h + 1) * HD, :], 0, keepdims=True) for h in range(heads)
        ]
        cot_low = cot.astype(LOW)
        query = q_in[at, :]
        q_parts = [query * pick[h : h + 1, :] for h in range(heads)]
        g_parts = [cot_low * pick[h : h + 1, :] for h in range(heads)]
        logs = lse[i]

        def inner(j, total):
            here = rows_of(j)
            keys, values = k_in[here, :], v_in[here, :]
            allowed = allowed_pairs(i, j, begin_row)
            key_part = jnp.zeros((QB, width), F32)
            value_part = jnp.zeros((QB, width), F32)
            for h in range(heads):
                scores = jnp.where(allowed, dot(keys, q_parts[h], 1, 1), -1000000000.0)
                prob = jnp.exp(scores - logs[h : h + 1, :])
                slope = dot(values, g_parts[h], 1, 1)
                back = (prob * (slope - deltas[h])).astype(LOW)
                key_part = key_part + dot(back, q_parts[h], 1, 0)
                value_part = value_part + dot(prob.astype(LOW), g_parts[h], 1, 0)
                total = total + dot(back, keys * pick[h : h + 1, :], 0, 0)
            key_sum[here, :] += key_part
            value_sum[here, :] += value_part
            return total

        total = lax.fori_loop(info[i], i + 1, inner, jnp.zeros((QB, width), F32))
        total = total * HD ** (-0.5)
        grad[at, :width] = spin(total, cos_t[at, :], sin_t[at, :], lane, True).astype(LOW)
        return carry

    def blank(i, carry):
        grad[rows_of(i), :width] = jnp.zeros((QB, width), LOW)
        return carry

    lax.fori_loop(0, count, block, 0)
    lax.fori_loop(count, blocks, blank, 0)

    def finish(i, carry):
        at = rows_of(i)
        turned = spin(key_sum[at, :], cos_t[at, :], sin_t[at, :], lane, True)
        grad[at, width : 2 * width] = turned.astype(LOW)
        grad[at, 2 * width :] = value_sum[at, :].astype(LOW)
        return carry

    lax.fori_loop(0, blocks, finish, 0)


def attend(heads, info, qkv, cosine, sine, begin, pick):
    full = qkv.shape[0]
    width = heads * HD
    blocks = full // QB
    vmem = pl.BlockSpec(memory_space=pltpu.VMEM)
    flat = jax.ShapeDtypeStruct((full, width), LOW)
    return pl.pallas_call(
        functools.partial(forward_kernel, heads),
        out_shape=(flat, jax.ShapeDtypeStruct((blocks, 8, QB), F32), flat, flat, flat),
        in_specs=[pl.BlockSpec(memory_space=pltpu.SMEM)] + [vmem] * 5,
        out_specs=[vmem] * 5,
        scratch_shapes=[
            pltpu.VMEM((heads, blocks, QB, QB), F32),
            pltpu.VMEM((blocks, width, QB), LOW),
        ],
        compiler_params=pltpu.CompilerParams(vmem_limit_bytes=40 * 1024 * 1024),
        cost_estimate=pl.CostEstimate(
            flops=full * full * width * 2, bytes_accessed=full * width * 20, transcendentals=full * full
        ),
    )(info, qkv, cosine, sine, begin, pick)


def attend_back(heads, info, query, key, value, out, grad_out, lse, cosine, sine, begin, pick):
    full = query.shape[0]
    width = heads * HD
    vmem = pl.BlockSpec(memory_space=pltpu.VMEM)
    return pl.pallas_call(
        functools.partial(backward_kernel, heads),
        out_shape=jax.ShapeDtypeStruct((full, 3 * width), LOW),
        in_specs=[pl.BlockSpec(memory_space=pltpu.SMEM)] + [vmem] * 10,
        out_specs=vmem,
        scratch_shapes=[pltpu.VMEM((full, width), F32)] * 2,
        compiler_params=pltpu.CompilerParams(vmem_limit_bytes=40 * 1024 * 1024),
        cost_estimate=pl.CostEstimate(
            flops=full * full * width * 6, bytes_accessed=full * width * 20, transcendentals=full * full
        ),
    )(info, query, key, value, out, grad_out, lse, cosine, sine, begin, pick)


def swap(part, bit):
    size = lax.axis_size("tensor")
    return lax.ppermute(part, "tensor", [(i, i ^ bit) for i in range(size)])


def gather_group(part):
    size = lax.axis_size("tensor")
    me = lax.axis_index("tensor")
    rows, cols = part.shape
    whole = jnp.zeros((size, rows, cols), part.dtype)
    held = [(0, part)]
    bit = size // 2
    while bit:
        stacked = jnp.concatenate([block for _, block in held], 0) if len(held) > 1 else held[0][1]
        arrived = swap(stacked, bit)
        held = held + [
            (far ^ bit, arrived[n * rows : (n + 1) * rows]) for n, (far, _) in enumerate(held)
        ]
        bit //= 2
    for far, block in held:
        whole = lax.dynamic_update_slice(whole, block[None], (me ^ far, 0, 0))
    return whole.reshape(size * rows, cols)


def half_of(part, rows, bit, mine):
    me = lax.axis_index("tensor")
    digit = (me // bit) % 2
    digit = digit if mine else 1 - digit
    blocks = part.shape[0] // rows
    grouped = part.reshape(blocks // 2, 2, rows, part.shape[1])
    picked = lax.dynamic_index_in_dim(grouped, digit, 1, keepdims=False)
    return picked.reshape(blocks // 2 * rows, part.shape[1])


def scatter_rest(total, rows):
    size = lax.axis_size("tensor")
    bit = 2
    while bit < size:
        away = half_of(total, rows, bit, False).astype(LOW)
        total = half_of(total, rows, bit, True) + swap(away, bit).astype(F32)
        bit *= 2
    return total


def split_three(values):
    high = lax.reduce_precision(values, 8, 7)
    rest = values - high
    middle = lax.reduce_precision(rest, 8, 7)
    return jnp.concatenate([high, middle, rest - middle], 0).astype(LOW)


def by_kind(part, heads):
    lead = part.shape[:-1]
    return jnp.swapaxes(part.reshape(lead + (heads, 3, HD)), -3, -2).reshape(lead + (-1,))


def by_head(part, heads):
    lead = part.shape[:-1]
    return jnp.swapaxes(part.reshape(lead + (3, heads, HD)), -3, -2).reshape(lead + (-1,))


def sum_over_groups(grad):
    return lax.psum_scatter(grad.astype(LOW), "dp", scatter_dimension=0, tiled=True).astype(F32)


def adamw(weight, grad, first, second, rate, decay):
    first_new = 0.9 * first + 0.1 * grad
    second_new = 0.999 * second + 0.001 * grad * grad
    moment_hat = first_new / (1.0 - 0.9**STEP)
    square_hat = second_new / (1.0 - 0.999**STEP)
    weight_new = weight - rate * (moment_hat / (jnp.sqrt(square_hat) + 1e-08) + decay * weight)
    return (weight_new, first_new, second_new)


def shards(
    hidden_in,
    grad_out,
    seq_lengths,
    qkv_weight,
    qkv_first,
    qkv_second,
    dense_weight,
    dense_first,
    dense_second,
    up_weight,
    up_first,
    up_second,
    down_weight,
    down_first,
    down_second,
    qkv_bias,
    qkv_bias_first,
    qkv_bias_second,
    up_bias,
    up_bias_first,
    up_bias_second,
    vectors,
    vectors_first,
    vectors_second,
):
    rows = hidden_in.shape[0]
    full = rows * lax.axis_size("tensor")
    offset = lax.axis_index("tensor") * rows
    groups = lax.axis_size("dp")
    width = dense_weight.shape[0]
    heads = width // HD
    hidden = up_weight.shape[1]
    begin, position, live, used = layout(seq_lengths[0])
    blocks = full // QB
    info = jnp.concatenate([begin[::QB] // QB, used[None], (used[None] + QB - 1) // QB])
    info = info.astype(jnp.int32)
    begin_rows = jnp.broadcast_to(begin.reshape(blocks, 1, QB), (blocks, 8, QB))
    cosine, sine = turn_tables(position)
    pick = (jnp.arange(width)[None, :] // HD == jnp.arange(8)[:, None]).astype(LOW)
    x_group = gather_group(hidden_in)
    here = lax.dynamic_slice_in_dim(live, offset, rows)
    dy_local = jnp.where(here[:, None], grad_out, jnp.zeros((), LOW))
    dy_group = gather_group(dy_local)

    shard = qkv_weight.shape[0]
    small = jnp.concatenate([qkv_bias, up_bias, vectors.reshape(-1)], 0)
    count = small.shape[0]
    wide = 3 * width
    extra = -(-3 * count // (16 * wide)) * 16
    packed = jnp.pad(split_three(small), (0, extra * wide - 3 * count)).reshape(extra, wide)
    sent = jnp.concatenate([by_kind(qkv_weight.astype(LOW), heads), packed], 0)
    got = lax.all_gather(sent, "dp", axis=0)
    w_qkv = got[:, :shard].reshape(groups * shard, wide)
    terms = got[:, shard:].reshape(groups, extra * wide)[:, : 3 * count].astype(F32)
    terms = terms.reshape(groups, 3, count).sum(1)
    n_bias, n_up = qkv_bias.shape[0], up_bias.shape[0]
    b_qkv = by_kind(terms[:, :n_bias].reshape(-1), heads)
    b_up = terms[:, n_bias : n_bias + n_up].reshape(-1)
    vecs = jnp.swapaxes(terms[:, n_bias + n_up :].reshape(groups, 6, -1), 0, 1).reshape(6, -1)
    w_up = lax.all_gather(up_weight.astype(LOW), "dp", axis=0, tiled=True)
    w_out = lax.all_gather(
        jnp.concatenate([down_weight.astype(LOW).T, dense_weight.astype(LOW).T], 1),
        "dp",
        axis=0,
        tiled=True,
    )

    def normalized(values):
        values = values.astype(F32)
        center = values - jnp.mean(values, -1, keepdims=True)
        scale = lax.rsqrt(jnp.mean(center * center, -1, keepdims=True) + 1e-05)
        return (center * scale, scale)

    unit, _ = normalized(x_group)
    norm_one = (unit * vecs[0] + vecs[1]).astype(LOW)
    norm_two = (unit * vecs[2] + vecs[3]).astype(LOW)
    qkv = dot(norm_one, w_qkv, 1, 0) + b_qkv
    attended, lse, query, key, value = attend(heads, info, qkv, cosine, sine, begin_rows, pick)
    upward = dot(norm_two, w_up, 1, 0) + b_up
    share = 0.5 * (1.0 + lax.erf(upward * math.sqrt(0.5)))
    activated = (upward * share).astype(LOW)
    slope = share + upward * jnp.exp(-0.5 * upward * upward) * (1.0 / math.sqrt(2.0 * math.pi))
    activated, slope = lax.optimization_barrier((activated, slope.astype(LOW)))
    inner = jnp.concatenate([activated, attended], 1)
    mixed_away = dot(half_of(inner, rows, 1, False), w_out, 1, 1).astype(LOW)
    mixed = dot(half_of(inner, rows, 1, True), w_out, 1, 1) + swap(mixed_away, 1).astype(F32)
    mixed = scatter_rest(mixed, rows)
    hidden_out = (hidden_in.astype(F32) + mixed + vecs[4] + vecs[5]).astype(LOW)

    grad_attended = dot(dy_group, w_out[:, hidden:], 1, 0).astype(LOW)
    grad_upward = (dot(dy_group, w_out[:, :hidden], 1, 0) * slope).astype(LOW)
    g_out = sum_over_groups(dot(dy_group, inner, 0, 0))
    g_up = sum_over_groups(dot(norm_two, grad_upward, 0, 0))
    grad_up_bias = jnp.sum(grad_upward.astype(F32), 0)
    grad_norm_two = dot(grad_upward, w_up, 1, 1)
    grad_qkv = attend_back(
        heads, info, query, key, value, attended, grad_attended, lse, cosine, sine, begin_rows, pick
    )
    grad_qkv_bias = jnp.sum(grad_qkv.astype(F32), 0)
    grad_qkv_weight = dot(norm_one, grad_qkv, 0, 0)
    grad_norm_one = dot(grad_qkv, w_qkv, 1, 1)
    error = grad_norm_one * vecs[0] + grad_norm_two * vecs[2]
    error_away = half_of(error, rows, 1, False).astype(LOW)
    error = half_of(error, rows, 1, True) + swap(error_away, 1).astype(F32)
    error = scatter_rest(error, rows)
    unit_here, scale_here = normalized(hidden_in)
    mean_error = jnp.mean(error, -1, keepdims=True)
    mean_both = jnp.mean(error * unit_here, -1, keepdims=True)
    dy_float = dy_local.astype(F32)
    hidden_grad = dy_float + scale_here * (error - mean_error - unit_here * mean_both)

    bias_grad = jnp.sum(dy_float, 0)
    grad_vectors = jnp.stack(
        [
            jnp.sum(grad_norm_one * unit, 0),
            jnp.sum(grad_norm_one, 0),
            jnp.sum(grad_norm_two * unit, 0),
            jnp.sum(grad_norm_two, 0),
            bias_grad,
            bias_grad,
        ],
        0,
    )
    grad_small = jnp.concatenate(
        [
            by_head(grad_qkv_bias, heads).reshape(groups, -1),
            grad_up_bias.reshape(groups, -1),
            jnp.swapaxes(grad_vectors.reshape(6, groups, -1), 0, 1).reshape(groups, -1),
        ],
        1,
    )
    more = -(-count // (16 * wide)) * 16
    grad_small = jnp.pad(grad_small.astype(LOW), ((0, 0), (0, more * wide - count)))
    grad_sent = jnp.concatenate(
        [grad_qkv_weight.astype(LOW).reshape(groups, shard, wide), grad_small.reshape(groups, more, wide)], 1
    )
    arrived = sum_over_groups(grad_sent.reshape(groups * (shard + more), wide))
    g_qkv = by_head(arrived[:shard], heads)
    g_small = arrived[shard:].reshape(-1)
    g_qbias = g_small[:n_bias]
    g_ubias = g_small[n_bias : n_bias + n_up]
    grad_vec_shard = lax.psum(g_small[n_bias + n_up : count].reshape(6, -1), "tensor")
    g_down = g_out[:, :hidden].T
    g_dense = g_out[:, hidden:].T
    qkv_set = adamw(qkv_weight, g_qkv, qkv_first, qkv_second, 2.0 * (D // 2) ** (-0.5), 0.01)
    dense_set = adamw(
        dense_weight, g_dense, dense_first, dense_second, 2.0 * (D // 16) ** (-0.5), 0.01
    )
    up_set = adamw(up_weight, g_up, up_first, up_second, 2.0 * D ** (-0.5), 0.01)
    down_set = adamw(down_weight, g_down, down_first, down_second, 2.0 * FF ** (-0.5), 0.01)
    qbias_set = adamw(qkv_bias, g_qbias, qkv_bias_first, qkv_bias_second, 0.6, 0.0)
    ubias_set = adamw(up_bias, g_ubias, up_bias_first, up_bias_second, 0.6, 0.0)
    vec_set = adamw(vectors, grad_vec_shard, vectors_first, vectors_second, 0.6, 0.0)
    return (
        hidden_out,
        hidden_grad,
        qkv_set[0],
        qkv_set[1],
        qkv_set[2],
        dense_set[0],
        dense_set[1],
        dense_set[2],
        up_set[0],
        up_set[1],
        up_set[2],
        down_set[0],
        down_set[1],
        down_set[2],
        qbias_set[0],
        qbias_set[1],
        qbias_set[2],
        ubias_set[0],
        ubias_set[1],
        ubias_set[2],
        vec_set[0],
        vec_set[1],
        vec_set[2],
    )


def solution(mesh):
    in_specs = (
        P(("dp", "tensor"), None),
        P(("dp", "tensor"), None),
        P("dp", None),
        P("dp", "tensor"),
        P("dp", "tensor"),
        P("dp", "tensor"),
        P("tensor", "dp"),
        P("tensor", "dp"),
        P("tensor", "dp"),
        P("dp", "tensor"),
        P("dp", "tensor"),
        P("dp", "tensor"),
        P("tensor", "dp"),
        P("tensor", "dp"),
        P("tensor", "dp"),
        P(("tensor", "dp")),
        P(("tensor", "dp")),
        P(("tensor", "dp")),
        P(("tensor", "dp")),
        P(("tensor", "dp")),
        P(("tensor", "dp")),
        P(None, "dp"),
        P(None, "dp"),
        P(None, "dp"),
    )
    out_specs = (
        P(("dp", "tensor"), None),
        P(("dp", "tensor"), None),
        P("dp", "tensor"),
        P("dp", "tensor"),
        P("dp", "tensor"),
        P("tensor", "dp"),
        P("tensor", "dp"),
        P("tensor", "dp"),
        P("dp", "tensor"),
        P("dp", "tensor"),
        P("dp", "tensor"),
        P("tensor", "dp"),
        P("tensor", "dp"),
        P("tensor", "dp"),
        P(("tensor", "dp")),
        P(("tensor", "dp")),
        P(("tensor", "dp")),
        P(("tensor", "dp")),
        P(("tensor", "dp")),
        P(("tensor", "dp")),
        P(None, "dp"),
        P(None, "dp"),
        P(None, "dp"),
    )
    return jax.shard_map(shards, mesh=mesh, in_specs=in_specs, out_specs=out_specs, check_vma=False)
```

```python
import functools
import math

import jax
import jax.numpy as jnp
from jax import lax
from jax.experimental import pallas as pl
from jax.experimental.pallas import tpu as pltpu
from jax.sharding import PartitionSpec as P

D = 1024
HD = 64
ROT = 16
FF = 4096
TOK_DEV = 2048
SEQS = 4
STEP = 10
QB = 256
LOW = jnp.bfloat16
F32 = jnp.float32


def dims(a, b):
    return (((a,), (b,)), ((), ()))


def dot(left, right, a, b):
    return lax.dot_general(left, right, dims(a, b), preferred_element_type=F32)


def layout(lengths):
    ends = jnp.cumsum(lengths)
    starts = ends - lengths
    place = jnp.arange(TOK_DEV, dtype=jnp.int32)
    segment = jnp.sum((place[:, None] >= ends[None, :]).astype(jnp.int32), 1)
    slots = jnp.arange(SEQS, dtype=jnp.int32)
    begin = jnp.sum(jnp.where(segment[:, None] == slots[None, :], starts[None, :], 0), 1)
    begin = jnp.where(segment == SEQS, ends[SEQS - 1], begin)
    return (begin, place - begin, segment < SEQS, ends[SEQS - 1])


def turn_tables(position):
    half = ROT // 2
    freq = jnp.exp(-math.log(10000.0) * jnp.arange(half, dtype=F32) * 2.0 / ROT)
    turn = freq[:, None] * position.astype(F32)[None, :]
    lane = jnp.arange(128) % HD
    pick = (lane[None, :] % half == jnp.arange(half)[:, None]) & (lane[None, :] < ROT)
    sign = jnp.where(lane < half, -1.0, 1.0)
    spread = functools.partial(jnp.einsum, "ft,fc->tc", precision=lax.Precision.HIGHEST)
    cosine = spread(jnp.cos(turn), pick.astype(F32)) + (lane >= ROT).astype(F32)
    sine = spread(jnp.sin(turn), pick.astype(F32) * sign)
    return (cosine, sine)


def spin(part, cosine, sine, lane, back):
    half = ROT // 2
    width = part.shape[1]
    copies = width // 128
    cos_w = jnp.concatenate([cosine] * copies, 1)
    sin_w = jnp.concatenate([sine] * copies, 1)
    other = jnp.where(
        lane % HD < half, pltpu.roll(part, width - half, 1), pltpu.roll(part, half, 1)
    )
    return part * cos_w - other * sin_w if back else part * cos_w + other * sin_w


def allowed_pairs(i, j, begin_row):
    key_place = j * QB + lax.broadcasted_iota(jnp.int32, (QB, QB), 0)
    query_place = i * QB + lax.broadcasted_iota(jnp.int32, (QB, QB), 1)
    return (key_place >= begin_row) & (key_place <= query_place)


def rows_of(i):
    return pl.ds(pl.multiple_of(i * QB, QB), QB)


def forward_kernel(
    heads, info, qkv, cos_t, sin_t, begin, pick, out, lse, q_out, k_out, v_out, score, v_turn
):
    width = heads * HD
    blocks = qkv.shape[0] // QB
    lane = lax.broadcasted_iota(jnp.int32, (QB, width), 1)
    used = info[blocks]

    def prepare(i, carry):
        at = rows_of(i)
        cosine, sine = cos_t[at, :], sin_t[at, :]
        query = spin(qkv[at, :width], cosine, sine, lane, False).astype(LOW)
        q_out[at, :] = (query.astype(F32) * HD ** (-0.5)).astype(LOW)
        k_out[at, :] = spin(qkv[at, width : 2 * width], cosine, sine, lane, False).astype(LOW)
        value = qkv[at, 2 * width :]
        v_out[at, :] = value.astype(LOW)
        v_turn[i] = value.T.astype(LOW)
        return carry

    lax.fori_loop(0, blocks, prepare, 0)

    def block(i, carry):
        at = rows_of(i)
        low = info[i]
        begin_row = begin[i][0:1]
        query = q_out[at, :]
        parts = [query * pick[h : h + 1, :] for h in range(heads)]

        def first(j, peaks):
            keys = k_out[rows_of(j), :]
            allowed = allowed_pairs(i, j, begin_row)
            new = []
            for h in range(heads):
                value = jnp.where(allowed, dot(keys, parts[h], 1, 1), -1000000000.0)
                score[h, j] = value
                new.append(jnp.maximum(peaks[h], jnp.max(value, 0, keepdims=True)))
            return tuple(new)

        peaks = lax.fori_loop(
            low, i + 1, first, tuple(jnp.full((1, QB), -2e9, F32) for _ in range(heads))
        )

        def second(j, state):
            totals, sums = state
            new_totals, new_sums = [], []
            for h in range(heads):
                prob = jnp.exp(score[h, j] - peaks[h])
                new_sums.append(sums[h] + jnp.sum(prob, 0, keepdims=True))
                v_part = v_turn[j, h * HD : (h + 1) * HD, :]
                new_totals.append(totals[h] + dot(v_part, prob.astype(LOW), 1, 0))
            return (tuple(new_totals), tuple(new_sums))

        totals, sums = lax.fori_loop(
            low,
            i + 1,
            second,
            (
                tuple(jnp.zeros((HD, QB), F32) for _ in range(heads)),
                tuple(jnp.zeros((1, QB), F32) for _ in range(heads)),
            ),
        )
        live = (i * QB + lax.broadcasted_iota(jnp.int32, (1, QB), 1) < used).astype(F32)
        result = jnp.concatenate([totals[h] * (live / sums[h]) for h in range(heads)], 0)
        out[at, :] = result.T.astype(LOW)
        logs = [peaks[h] + jnp.log(sums[h]) for h in range(heads)]
        lse[i] = jnp.concatenate(logs + [jnp.zeros((8 - heads, QB), F32)], 0)
        return carry

    def blank(i, carry):
        out[rows_of(i), :] = jnp.zeros((QB, width), LOW)
        lse[i] = jnp.zeros((8, QB), F32)
        return carry

    count = info[blocks + 1]
    lax.fori_loop(0, count, block, 0)
    lax.fori_loop(count, blocks, blank, 0)


def backward_kernel(
    heads, info, q_in, k_in, v_in, out, grad_out, lse, cos_t, sin_t, begin, pick, grad, key_sum, value_sum
):
    width = heads * HD
    blocks = q_in.shape[0] // QB
    lane = lax.broadcasted_iota(jnp.int32, (QB, width), 1)
    used = info[blocks]
    count = info[blocks + 1]
    key_sum[...] = jnp.zeros_like(key_sum)
    value_sum[...] = jnp.zeros_like(value_sum)

    def block(i, carry):
        at = rows_of(i)
        begin_row = begin[i][0:1]
        row = i * QB + lax.broadcasted_iota(jnp.int32, (QB, width), 0)
        cot = jnp.where(row < used, grad_out[at, :].astype(F32), 0.0)
        spread = (cot * out[at, :].astype(F32)).T
        deltas = [
            jnp.sum(spread[h * HD : (h + 1) * HD, :], 0, keepdims=True) for h in range(heads)
        ]
        cot_low = cot.astype(LOW)
        query = q_in[at, :]
        q_parts = [query * pick[h : h + 1, :] for h in range(heads)]
        g_parts = [cot_low * pick[h : h + 1, :] for h in range(heads)]
        logs = lse[i]

        def inner(j, total):
            here = rows_of(j)
            keys, values = k_in[here, :], v_in[here, :]
            allowed = allowed_pairs(i, j, begin_row)
            key_part = jnp.zeros((QB, width), F32)
            value_part = jnp.zeros((QB, width), F32)
            for h in range(heads):
                scores = jnp.where(allowed, dot(keys, q_parts[h], 1, 1), -1000000000.0)
                prob = jnp.exp(scores - logs[h : h + 1, :])
                slope = dot(values, g_parts[h], 1, 1)
                back = (prob * (slope - deltas[h])).astype(LOW)
                key_part = key_part + dot(back, q_parts[h], 1, 0)
                value_part = value_part + dot(prob.astype(LOW), g_parts[h], 1, 0)
                total = total + dot(back, keys * pick[h : h + 1, :], 0, 0)
            key_sum[here, :] += key_part
            value_sum[here, :] += value_part
            return total

        total = lax.fori_loop(info[i], i + 1, inner, jnp.zeros((QB, width), F32))
        total = total * HD ** (-0.5)
        grad[at, :width] = spin(total, cos_t[at, :], sin_t[at, :], lane, True).astype(LOW)
        return carry

    def blank(i, carry):
        grad[rows_of(i), :width] = jnp.zeros((QB, width), LOW)
        return carry

    lax.fori_loop(0, count, block, 0)
    lax.fori_loop(count, blocks, blank, 0)

    def finish(i, carry):
        at = rows_of(i)
        turned = spin(key_sum[at, :], cos_t[at, :], sin_t[at, :], lane, True)
        grad[at, width : 2 * width] = turned.astype(LOW)
        grad[at, 2 * width :] = value_sum[at, :].astype(LOW)
        return carry

    lax.fori_loop(0, blocks, finish, 0)


def attend(heads, info, qkv, cosine, sine, begin, pick):
    full = qkv.shape[0]
    width = heads * HD
    blocks = full // QB
    vmem = pl.BlockSpec(memory_space=pltpu.VMEM)
    flat = jax.ShapeDtypeStruct((full, width), LOW)
    return pl.pallas_call(
        functools.partial(forward_kernel, heads),
        out_shape=(flat, jax.ShapeDtypeStruct((blocks, 8, QB), F32), flat, flat, flat),
        in_specs=[pl.BlockSpec(memory_space=pltpu.SMEM)] + [vmem] * 5,
        out_specs=[vmem] * 5,
        scratch_shapes=[
            pltpu.VMEM((heads, blocks, QB, QB), F32),
            pltpu.VMEM((blocks, width, QB), LOW),
        ],
        compiler_params=pltpu.CompilerParams(vmem_limit_bytes=40 * 1024 * 1024),
        cost_estimate=pl.CostEstimate(
            flops=full * full * width * 2, bytes_accessed=full * width * 20, transcendentals=full * full
        ),
    )(info, qkv, cosine, sine, begin, pick)


def attend_back(heads, info, query, key, value, out, grad_out, lse, cosine, sine, begin, pick):
    full = query.shape[0]
    width = heads * HD
    vmem = pl.BlockSpec(memory_space=pltpu.VMEM)
    return pl.pallas_call(
        functools.partial(backward_kernel, heads),
        out_shape=jax.ShapeDtypeStruct((full, 3 * width), LOW),
        in_specs=[pl.BlockSpec(memory_space=pltpu.SMEM)] + [vmem] * 10,
        out_specs=vmem,
        scratch_shapes=[pltpu.VMEM((full, width), F32)] * 2,
        compiler_params=pltpu.CompilerParams(vmem_limit_bytes=40 * 1024 * 1024),
        cost_estimate=pl.CostEstimate(
            flops=full * full * width * 6, bytes_accessed=full * width * 20, transcendentals=full * full
        ),
    )(info, query, key, value, out, grad_out, lse, cosine, sine, begin, pick)


def swap(part, bit, axis="tensor"):
    size = lax.axis_size(axis)
    return lax.ppermute(part, axis, [(i, i ^ bit) for i in range(size)])


def gather_group(part, axis="tensor"):
    size = lax.axis_size(axis)
    me = lax.axis_index(axis)
    rows, cols = part.shape
    whole = jnp.zeros((size, rows, cols), part.dtype)
    held = [(0, part)]
    bit = size // 2
    while bit:
        stacked = jnp.concatenate([block for _, block in held], 0) if len(held) > 1 else held[0][1]
        arrived = swap(stacked, bit, axis)
        held = held + [
            (far ^ bit, arrived[n * rows : (n + 1) * rows]) for n, (far, _) in enumerate(held)
        ]
        bit //= 2
    for far, block in held:
        whole = lax.dynamic_update_slice(whole, block[None], (me ^ far, 0, 0))
    return whole.reshape(size * rows, cols)


def half_of(part, rows, bit, mine, axis="tensor"):
    me = lax.axis_index(axis)
    digit = (me // bit) % 2
    digit = digit if mine else 1 - digit
    blocks = part.shape[0] // rows
    grouped = part.reshape(blocks // 2, 2, rows, part.shape[1])
    picked = lax.dynamic_index_in_dim(grouped, digit, 1, keepdims=False)
    return picked.reshape(blocks // 2 * rows, part.shape[1])


def scatter_rest(total, rows, axis="tensor", bit=2):
    size = lax.axis_size(axis)
    while bit < size:
        away = half_of(total, rows, bit, False, axis).astype(LOW)
        total = half_of(total, rows, bit, True, axis) + swap(away, bit, axis).astype(F32)
        bit *= 2
    return total


def split_three(values):
    high = lax.reduce_precision(values, 8, 7)
    rest = values - high
    middle = lax.reduce_precision(rest, 8, 7)
    return jnp.concatenate([high, middle, rest - middle], 0).astype(LOW)


def by_kind(part, heads):
    lead = part.shape[:-1]
    return jnp.swapaxes(part.reshape(lead + (heads, 3, HD)), -3, -2).reshape(lead + (-1,))


def by_head(part, heads):
    lead = part.shape[:-1]
    return jnp.swapaxes(part.reshape(lead + (3, heads, HD)), -3, -2).reshape(lead + (-1,))


def sum_over_groups(grad):
    return lax.psum_scatter(grad.astype(LOW), "dp", scatter_dimension=0, tiled=True).astype(F32)


def adamw(weight, grad, first, second, rate, decay):
    first_new = 0.9 * first + 0.1 * grad
    second_new = 0.999 * second + 0.001 * grad * grad
    moment_hat = first_new / (1.0 - 0.9**STEP)
    square_hat = second_new / (1.0 - 0.999**STEP)
    weight_new = weight - rate * (moment_hat / (jnp.sqrt(square_hat) + 1e-08) + decay * weight)
    return (weight_new, first_new, second_new)


def shards(
    hidden_in,
    grad_out,
    seq_lengths,
    qkv_weight,
    qkv_first,
    qkv_second,
    dense_weight,
    dense_first,
    dense_second,
    up_weight,
    up_first,
    up_second,
    down_weight,
    down_first,
    down_second,
    qkv_bias,
    qkv_bias_first,
    qkv_bias_second,
    up_bias,
    up_bias_first,
    up_bias_second,
    vectors,
    vectors_first,
    vectors_second,
):
    rows = hidden_in.shape[0]
    full = rows * lax.axis_size("tensor")
    offset = lax.axis_index("tensor") * rows
    groups = lax.axis_size("dp")
    width = dense_weight.shape[0]
    heads = width // HD
    hidden = up_weight.shape[1]
    begin, position, live, used = layout(seq_lengths[0])
    blocks = full // QB
    info = jnp.concatenate([begin[::QB] // QB, used[None], (used[None] + QB - 1) // QB])
    info = info.astype(jnp.int32)
    begin_rows = jnp.broadcast_to(begin.reshape(blocks, 1, QB), (blocks, 8, QB))
    cosine, sine = turn_tables(position)
    pick = (jnp.arange(width)[None, :] // HD == jnp.arange(8)[:, None]).astype(LOW)
    x_group = gather_group(hidden_in)
    here = lax.dynamic_slice_in_dim(live, offset, rows)
    dy_local = jnp.where(here[:, None], grad_out, jnp.zeros((), LOW))
    dy_group = gather_group(dy_local)

    shard = qkv_weight.shape[0]
    small = jnp.concatenate([qkv_bias, up_bias, vectors.reshape(-1)], 0)
    count = small.shape[0]
    wide = 3 * width
    extra = -(-3 * count // (16 * wide)) * 16
    packed = jnp.pad(split_three(small), (0, extra * wide - 3 * count)).reshape(extra, wide)
    sent = jnp.concatenate([by_kind(qkv_weight.astype(LOW), heads), packed], 0)
    got = lax.all_gather(sent, "dp", axis=0)
    w_qkv = got[:, :shard].reshape(groups * shard, wide)
    terms = got[:, shard:].reshape(groups, extra * wide)[:, : 3 * count].astype(F32)
    terms = terms.reshape(groups, 3, count).sum(1)
    n_bias, n_up = qkv_bias.shape[0], up_bias.shape[0]
    b_qkv = by_kind(terms[:, :n_bias].reshape(-1), heads)
    b_up = terms[:, n_bias : n_bias + n_up].reshape(-1)
    vecs = jnp.swapaxes(terms[:, n_bias + n_up :].reshape(groups, 6, -1), 0, 1).reshape(6, -1)
    w_up = lax.all_gather(up_weight.astype(LOW), "dp", axis=0, tiled=True)
    w_out = gather_group(
        jnp.concatenate([down_weight.astype(LOW).T, dense_weight.astype(LOW).T], 1), "dp"
    )

    def normalized(values):
        values = values.astype(F32)
        center = values - jnp.mean(values, -1, keepdims=True)
        scale = lax.rsqrt(jnp.mean(center * center, -1, keepdims=True) + 1e-05)
        return (center * scale, scale)

    unit, _ = normalized(x_group)
    norm_one = (unit * vecs[0] + vecs[1]).astype(LOW)
    norm_two = (unit * vecs[2] + vecs[3]).astype(LOW)
    qkv = dot(norm_one, w_qkv, 1, 0) + b_qkv
    attended, lse, query, key, value = attend(heads, info, qkv, cosine, sine, begin_rows, pick)
    upward = dot(norm_two, w_up, 1, 0) + b_up
    share = 0.5 * (1.0 + lax.erf(upward * math.sqrt(0.5)))
    activated = (upward * share).astype(LOW)
    slope = share + upward * jnp.exp(-0.5 * upward * upward) * (1.0 / math.sqrt(2.0 * math.pi))
    activated, slope = lax.optimization_barrier((activated, slope.astype(LOW)))
    inner = jnp.concatenate([activated, attended], 1)
    mixed_away = dot(half_of(inner, rows, 1, False), w_out, 1, 1).astype(LOW)
    mixed = dot(half_of(inner, rows, 1, True), w_out, 1, 1) + swap(mixed_away, 1).astype(F32)
    mixed = scatter_rest(mixed, rows)
    hidden_out = (hidden_in.astype(F32) + mixed + vecs[4] + vecs[5]).astype(LOW)

    grad_attended = dot(dy_group, w_out[:, hidden:], 1, 0).astype(LOW)
    grad_upward = (dot(dy_group, w_out[:, :hidden], 1, 0) * slope).astype(LOW)
    part_up = dot(norm_two, grad_upward, 0, 0).astype(LOW)
    part_out = dot(dy_group, inner, 0, 0)
    part_up, part_out, grad_attended = lax.optimization_barrier((part_up, part_out, grad_attended))
    g_up = sum_over_groups(part_up)
    g_out = scatter_rest(part_out, shard, "dp", 1)
    grad_up_bias = jnp.sum(grad_upward.astype(F32), 0)
    grad_norm_two = dot(grad_upward, w_up, 1, 1)
    grad_qkv = attend_back(
        heads, info, query, key, value, attended, grad_attended, lse, cosine, sine, begin_rows, pick
    )
    grad_qkv_bias = jnp.sum(grad_qkv.astype(F32), 0)
    grad_qkv_weight = dot(norm_one, grad_qkv, 0, 0)
    grad_norm_one = dot(grad_qkv, w_qkv, 1, 1)
    error = grad_norm_one * vecs[0] + grad_norm_two * vecs[2]
    error_away = half_of(error, rows, 1, False).astype(LOW)
    error = half_of(error, rows, 1, True) + swap(error_away, 1).astype(F32)
    error = scatter_rest(error, rows)
    unit_here, scale_here = normalized(hidden_in)
    mean_error = jnp.mean(error, -1, keepdims=True)
    mean_both = jnp.mean(error * unit_here, -1, keepdims=True)
    dy_float = dy_local.astype(F32)
    hidden_grad = dy_float + scale_here * (error - mean_error - unit_here * mean_both)

    bias_grad = jnp.sum(dy_float, 0)
    grad_vectors = jnp.stack(
        [
            jnp.sum(grad_norm_one * unit, 0),
            jnp.sum(grad_norm_one, 0),
            jnp.sum(grad_norm_two * unit, 0),
            jnp.sum(grad_norm_two, 0),
            bias_grad,
            bias_grad,
        ],
        0,
    )
    grad_small = jnp.concatenate(
        [
            by_head(grad_qkv_bias, heads).reshape(groups, -1),
            grad_up_bias.reshape(groups, -1),
            jnp.swapaxes(grad_vectors.reshape(6, groups, -1), 0, 1).reshape(groups, -1),
        ],
        1,
    )
    more = -(-count // (16 * wide)) * 16
    grad_small = jnp.pad(grad_small.astype(LOW), ((0, 0), (0, more * wide - count)))
    grad_sent = jnp.concatenate(
        [grad_qkv_weight.astype(LOW).reshape(groups, shard, wide), grad_small.reshape(groups, more, wide)], 1
    )
    arrived = sum_over_groups(grad_sent.reshape(groups * (shard + more), wide))
    g_qkv = by_head(arrived[:shard], heads)
    g_small = arrived[shard:].reshape(-1)
    g_qbias = g_small[:n_bias]
    g_ubias = g_small[n_bias : n_bias + n_up]
    grad_vec_shard = lax.psum(g_small[n_bias + n_up : count].reshape(6, -1), "tensor")
    g_down = g_out[:, :hidden].T
    g_dense = g_out[:, hidden:].T
    qkv_set = adamw(qkv_weight, g_qkv, qkv_first, qkv_second, 2.0 * (D // 2) ** (-0.5), 0.01)
    dense_set = adamw(
        dense_weight, g_dense, dense_first, dense_second, 2.0 * (D // 16) ** (-0.5), 0.01
    )
    up_set = adamw(up_weight, g_up, up_first, up_second, 2.0 * D ** (-0.5), 0.01)
    down_set = adamw(down_weight, g_down, down_first, down_second, 2.0 * FF ** (-0.5), 0.01)
    qbias_set = adamw(qkv_bias, g_qbias, qkv_bias_first, qkv_bias_second, 0.6, 0.0)
    ubias_set = adamw(up_bias, g_ubias, up_bias_first, up_bias_second, 0.6, 0.0)
    vec_set = adamw(vectors, grad_vec_shard, vectors_first, vectors_second, 0.6, 0.0)
    return (
        hidden_out,
        hidden_grad,
        qkv_set[0],
        qkv_set[1],
        qkv_set[2],
        dense_set[0],
        dense_set[1],
        dense_set[2],
        up_set[0],
        up_set[1],
        up_set[2],
        down_set[0],
        down_set[1],
        down_set[2],
        qbias_set[0],
        qbias_set[1],
        qbias_set[2],
        ubias_set[0],
        ubias_set[1],
        ubias_set[2],
        vec_set[0],
        vec_set[1],
        vec_set[2],
    )


def solution(mesh):
    in_specs = (
        P(("dp", "tensor"), None),
        P(("dp", "tensor"), None),
        P("dp", None),
        P("dp", "tensor"),
        P("dp", "tensor"),
        P("dp", "tensor"),
        P("tensor", "dp"),
        P("tensor", "dp"),
        P("tensor", "dp"),
        P("dp", "tensor"),
        P("dp", "tensor"),
        P("dp", "tensor"),
        P("tensor", "dp"),
        P("tensor", "dp"),
        P("tensor", "dp"),
        P(("tensor", "dp")),
        P(("tensor", "dp")),
        P(("tensor", "dp")),
        P(("tensor", "dp")),
        P(("tensor", "dp")),
        P(("tensor", "dp")),
        P(None, "dp"),
        P(None, "dp"),
        P(None, "dp"),
    )
    out_specs = (
        P(("dp", "tensor"), None),
        P(("dp", "tensor"), None),
        P("dp", "tensor"),
        P("dp", "tensor"),
        P("dp", "tensor"),
        P("tensor", "dp"),
        P("tensor", "dp"),
        P("tensor", "dp"),
        P("dp", "tensor"),
        P("dp", "tensor"),
        P("dp", "tensor"),
        P("tensor", "dp"),
        P("tensor", "dp"),
        P("tensor", "dp"),
        P(("tensor", "dp")),
        P(("tensor", "dp")),
        P(("tensor", "dp")),
        P(("tensor", "dp")),
        P(("tensor", "dp")),
        P(("tensor", "dp")),
        P(None, "dp"),
        P(None, "dp"),
        P(None, "dp"),
    )
    return jax.shard_map(shards, mesh=mesh, in_specs=in_specs, out_specs=out_specs, check_vma=False)
```
